32 devices in a mesh: pack: 8 (over z, y), hist: 4 (over x, core).
Axes of the slice: x: 2, y: 2, z: 4, core: 2. Of those that a mesh axis runs over, the one named last changes fastest.
Arguments:
- queries: bfloat16 [8, 2048, 2048], P('pack', 'hist'), may hold values from -0.59765625 to 0.59765625
- keys: bfloat16 [8, 2048, 2048], P('pack', 'hist'), may hold values from -6 to 6
- values: bfloat16 [8, 2048, 2048], P('pack', 'hist'), may hold values from -6 to 6
- gates: bfloat16 [8, 2048, 2048], P('pack', 'hist'), may hold values from -6 to 6
- user_ids: int32 [8, 2048], P('pack', 'hist'), may hold values from 0 to 5, never falling along the last dimension, each value on 1 to 682 neighbouring positions
- forget_rate: float32 [16], replicated, may hold values from 0.0001 to 0.02
- norm_gain: float32 [2048], replicated, may hold values from 0.1 to 1.9
- w_out: bfloat16 [2048, 2048], P('pack'), may hold values from -0.125 to 0.125
Outputs:
- mixed: bfloat16 [8, 2048, 2048], P('pack', 'hist')
The draws below stay inside these ranges and needn't reach their ends.
Inputs may be any that keep to these rules, and one draw needn't show every extreme that they name: `user_ids`: in each window user ids never fall along the events; each user holds 1 to 682 consecutive events, and one user exactly 682.
All inputs are finite; a program needn't handle non-finite values.
Results may differ from the reference program's by a relative error of at most 0.0061.
Values may be sent and summed in bfloat16 or wider, within the bound.
A program may use at most 128 MiB of HBM per device.

```python
import math
import jax
import jax.numpy as jnp
import numpy as np
from jax import lax

D = 2048
HEADS = 16
HEAD_DIM = 128
GROUP = 128
USERS = 6
EVENTS = 2048
LONGEST = 682
WINDOWS = 8


def block_levels(own_key, shape, cuts, smallest, high):
    level, own = 1.0, jax.random.fold_in(own_key, 6)
    for dim, blocks in cuts:
        draws = jnp.exp(jax.random.uniform(jax.random.fold_in(own, dim), (blocks,), jnp.float32, smallest / len(cuts), high / len(cuts)))
        level = level * jnp.repeat(draws, shape[dim] // blocks).reshape([-1 if axis == dim else 1 for axis in range(len(shape))])
    return level


def profile(amount, total, most, slope):
    loads = [(1 << 20) // math.isqrt(rank ** slope) + 1 for rank in range(2, amount + 1)]
    rest, given = total - most - (amount - 1), [1] * (amount - 1)
    while rest > 0:
        movable = [i for i in range(amount - 1) if given[i] < most]
        whole, budget = sum([loads[i] for i in movable]), rest
        for i in movable:
            extra = min(most - given[i], max(1, budget * loads[i] // whole), rest)
            given[i] = given[i] + extra
            rest = rest - extra
    return np.array([most] + given)


def ragged(stream_key, number_of, total, most, slope):
    if number_of == 2:
        one = jax.random.randint(stream_key, (), max(1, total - most), min(most, total - 1) + 1)
        return jnp.stack([one, total - one])
    sizes = jnp.asarray(profile(number_of, total, most, slope), jnp.int32)
    couples = (number_of - 1) // 2
    giver, receiver = sizes[1:1 + 2 * couples:2], sizes[2:2 + 2 * couples:2]
    slack = jnp.minimum(giver - 1, most - receiver)
    shifted = jax.random.randint(jax.random.fold_in(stream_key, 1), (couples,), 0, 1 << 20) % (slack + 1)
    sizes = sizes.at[1:1 + 2 * couples:2].set(giver - shifted).at[2:2 + 2 * couples:2].set(receiver + shifted)
    return sizes[jax.random.permutation(jax.random.fold_in(stream_key, 2), number_of)]


def bell_draw(key, shape, deviation, most, split=(), kind=jnp.bfloat16):
    entries = jax.random.normal(key, shape, jnp.float32) * deviation
    if len(split) > 0:
        entries = block_levels(key, shape, split, -0.22, 0.18) * entries
    return jnp.clip(entries, min=-most, max=most).astype(kind)


def setup_inputs(seed: int = 0) -> dict:
    key_list = jax.random.split(jax.random.key(seed), 9)
    queries = bell_draw(key_list[0], (WINDOWS, EVENTS, D), 0.09, 0.59765625, ((0, 8), (1, 4)))
    keys = bell_draw(key_list[1], (WINDOWS, EVENTS, D), 1.0, 6.0, ((0, 8), (1, 4)))
    values = bell_draw(key_list[2], (WINDOWS, EVENTS, D), 1.0, 6.0, ((0, 8), (1, 4)))
    gates = bell_draw(key_list[3], (WINDOWS, EVENTS, D), 1.0, 6.0, ((0, 8), (1, 4)))
    user_ids = jax.vmap(lambda own: jnp.searchsorted(jnp.cumsum(ragged(own, USERS, EVENTS, LONGEST, 2)), jnp.arange(EVENTS), side="right"))(jax.random.split(key_list[4], WINDOWS)).reshape((WINDOWS, EVENTS)).astype(jnp.int32)
    forget_rate = jnp.clip(jnp.exp(jax.random.uniform(key_list[5], (HEADS,), jnp.float32, math.log(0.0001), math.log(0.02))), 0.0001, 0.02)
    norm_gain = jnp.clip(1.0 + 0.18 * jax.random.normal(key_list[6], (D,), jnp.float32), 0.1, 1.9)
    w_out = bell_draw(key_list[7], (D, D), D ** -0.5, 0.125, ((0, 8),))
    return dict(queries=queries, keys=keys, values=values, gates=gates, user_ids=user_ids, forget_rate=forget_rate, norm_gain=norm_gain, w_out=w_out)


def one_window(items, forget_rate, norm_gain, w_out):
    queries, keys, values, gates, user_ids = items
    blocks = EVENTS // GROUP
    log_decay = jnp.log1p(-forget_rate.astype(jnp.float32))
    prior = jnp.concatenate([jnp.full((1,), -1, jnp.int32), user_ids[:-1].astype(jnp.int32)])
    starts = (user_ids != prior).astype(jnp.int32)
    seg = user_ids.reshape(blocks, GROUP)
    start_blk = starts.reshape(blocks, GROUP)
    qf = queries.astype(jnp.float32).reshape(blocks, GROUP, HEADS, HEAD_DIM)
    kf = keys.astype(jnp.float32).reshape(blocks, GROUP, HEADS, HEAD_DIM)
    vf = values.astype(jnp.float32).reshape(blocks, GROUP, HEADS, HEAD_DIM)
    place = jnp.arange(GROUP, dtype=jnp.int32)
    diff = place[:, None] - place[None, :]
    causal = diff >= 0
    lag = jnp.where(causal, diff, 0).astype(jnp.float32)
    decay = jnp.exp(lag[None] * log_decay[:, None, None])
    same = seg[:, :, None] == seg[:, None, :]
    mask = jnp.logical_and(same, causal[None])
    scores = jnp.einsum('nthd,nshd->nhts', qf, kf)
    weights = jnp.where(mask[:, None], scores * decay[None], 0.0).astype(jnp.bfloat16)
    inner = jnp.einsum('nhts,nshd->nthd', weights.astype(jnp.float32), vf)
    last_user = seg[:, -1]
    tail = jnp.exp((GROUP - 1 - place).astype(jnp.float32)[None, :] * log_decay[:, None])
    keep_rows = (seg == last_user[:, None]).astype(jnp.float32)
    scaled = (kf * (keep_rows[:, :, None] * tail.T[None])[..., None]).astype(jnp.bfloat16)
    own = jnp.einsum('nshd,nshe->nhde', scaled.astype(jnp.float32), vf)
    any_start = lax.optimization_barrier(jnp.max(start_blk, axis=1)) > 0
    keep = jnp.where(any_start[:, None], 0.0, jnp.exp(GROUP * log_decay)[None, :])

    def advance(state, item):
        keep_c, own_c = item
        return (keep_c[:, None, None] * state + own_c, state)
    zero_state = jnp.zeros((HEADS, HEAD_DIM, HEAD_DIM), jnp.float32)
    final, entering = lax.scan(advance, zero_state, (keep, own))
    entering = entering.astype(jnp.bfloat16)
    open_run = (jnp.cumsum(start_blk, axis=1) == 0).astype(jnp.float32)
    reach = jnp.exp((place + 1).astype(jnp.float32)[:, None] * log_decay[None, :])
    factor = open_run[:, :, None] * reach[None]
    carried = jnp.einsum('nthd,nhde->nthe', qf, entering.astype(jnp.float32)) * factor[..., None]
    retained = (inner + carried).reshape(EVENTS, HEADS, HEAD_DIM)
    mean = lax.optimization_barrier(jnp.mean(retained, axis=2, keepdims=True))
    centred = retained - mean
    variance = lax.optimization_barrier(jnp.mean(centred * centred, axis=2, keepdims=True))
    normed = (centred * lax.rsqrt(variance + 1e-05)).reshape(EVENTS, D) * norm_gain.astype(jnp.float32)
    gated = (jax.nn.silu(gates.astype(jnp.float32)) * normed).astype(jnp.bfloat16)
    return jnp.dot(gated, w_out, preferred_element_type=jnp.float32).astype(jnp.bfloat16)

def reference(queries, keys, values, gates, user_ids, forget_rate, norm_gain, w_out):

    def per_window(items):
        return one_window(items, forget_rate, norm_gain, w_out)
    return lax.map(per_window, (queries, keys, values, gates, user_ids))
```

```python
import functools

import jax
import jax.numpy as jnp
from jax import lax
from jax.experimental import pallas as pl
from jax.experimental.pallas import tpu as pltpu
from jax.sharding import PartitionSpec as P

HEADS = 16
GROUP = 128


def passed_along(array, axis, by):
    size = lax.axis_size(axis)
    pairs = [(i, i + by) for i in range(size) if 0 <= i + by < size]
    return lax.ppermute(array, axis, pairs)


def carried_in(array, axis, combine, identity):
    size, here = (lax.axis_size(axis), lax.axis_index(axis))
    everything = jax.tree.map(lambda part: lax.all_gather(part, axis), array)
    start = jax.tree.map(
        lambda part, zero: jnp.broadcast_to(jnp.asarray(zero, part.dtype), part.shape),
        array,
        identity,
    )

    def hop(k, before):
        reached = k < here
        new = combine(before, jax.tree.map(lambda part: part[k], everything))
        return jax.tree.map(lambda a, b: jnp.where(reached, a, b), new, before)

    return lax.fori_loop(0, size, hop, start)


def combine_states(earlier, later):
    return (earlier[0] * later[0], later[0][:, None, None] * earlier[1] + later[1])


def local_any(queries, keys, values, gates, user_ids, forget_rate, norm_gain, w_out):
    length = queries.shape[1]
    width = queries.shape[2]
    head_dim = width // HEADS
    blocks = length // GROUP
    log_decay = jnp.log1p(-forget_rate)
    users = user_ids[0]
    before = passed_along(users[length - 1 :], "hist", 1)
    prior = jnp.concatenate([before, users[:-1]])
    place_all = jnp.arange(length, dtype=jnp.int32)
    forced = jnp.logical_and(lax.axis_index("hist") == 0, place_all == 0)
    starts = jnp.logical_or(users != prior, forced).astype(jnp.int32)
    seg = users.reshape(blocks, GROUP)
    start_blk = starts.reshape(blocks, GROUP)
    q_blk = queries[0].reshape(blocks, GROUP, HEADS, head_dim)
    k_blk = keys[0].reshape(blocks, GROUP, HEADS, head_dim)
    v_blk = values[0].reshape(blocks, GROUP, HEADS, head_dim)
    place = jnp.arange(GROUP, dtype=jnp.int32)
    diff = place[:, None] - place[None, :]
    causal = diff >= 0
    lag = jnp.where(causal, diff, 0).astype(jnp.float32)
    decay = jnp.exp(lag[None] * log_decay[:, None, None])
    mask = jnp.logical_and(seg[:, :, None] == seg[:, None, :], causal[None])
    scores = jnp.einsum("nthd,nshd->nhts", q_blk, k_blk, preferred_element_type=jnp.float32)
    weights = jnp.where(mask[:, None], scores * decay[None], 0.0).astype(jnp.bfloat16)
    inner = jnp.einsum("nhts,nshd->nthd", weights, v_blk, preferred_element_type=jnp.float32)
    tail = jnp.exp((GROUP - 1 - place).astype(jnp.float32)[None, :] * log_decay[:, None])
    keep_rows = (seg == seg[:, -1:]).astype(jnp.float32)
    scaled = (k_blk * (keep_rows[:, :, None] * tail.T[None])[..., None]).astype(jnp.bfloat16)
    own = jnp.einsum("nshd,nshe->nhde", scaled, v_blk, preferred_element_type=jnp.float32)
    any_start = jnp.max(start_blk, axis=1) > 0
    keep = jnp.where(any_start[:, None], 0.0, jnp.exp(GROUP * log_decay)[None, :])

    def advance(state, item):
        keep_c, own_c = item
        return (keep_c[:, None, None] * state + own_c, state)

    zero_state = jnp.zeros((HEADS, head_dim, head_dim), jnp.float32)
    local_final, local_enter = lax.scan(advance, zero_state, (keep, own))
    products = [jnp.ones((HEADS,), jnp.float32)]
    for c in range(blocks - 1):
        products.append(products[-1] * keep[c])
    keep_before = jnp.stack(products)
    keep_device = keep_before[-1] * keep[-1]
    identity = (
        jnp.ones((HEADS,), jnp.float32),
        jnp.zeros((HEADS, head_dim, head_dim), jnp.float32),
    )
    incoming = carried_in((keep_device, local_final), "hist", combine_states, identity)[1]
    entering = (local_enter + keep_before[:, :, None, None] * incoming[None]).astype(jnp.bfloat16)
    ahead = prior.reshape(blocks, GROUP)[:, :1]
    first = starts.reshape(blocks, GROUP)[:, :1]
    open_run = jnp.logical_and(seg == ahead, first == 0).astype(jnp.float32)
    reach = jnp.exp((place + 1).astype(jnp.float32)[:, None] * log_decay[None, :])
    factor = open_run[:, :, None] * reach[None]
    carried = (
        jnp.einsum("nthd,nhde->nthe", q_blk, entering, preferred_element_type=jnp.float32)
        * factor[..., None]
    )
    retained = (inner + carried).reshape(length, HEADS, head_dim)
    mean = jnp.mean(retained, axis=2, keepdims=True)
    centred = retained - mean
    variance = jnp.mean(centred * centred, axis=2, keepdims=True)
    normed = (centred * lax.rsqrt(variance + 1e-05)).reshape(length, width) * norm_gain
    gated = (jax.nn.silu(gates[0].astype(jnp.float32)) * normed).astype(jnp.bfloat16)
    mixed = jnp.dot(
        gated, lax.all_gather(w_out, "pack", axis=0, tiled=True), preferred_element_type=jnp.float32
    ).astype(jnp.bfloat16)
    return mixed[None]


HEAD_DIM = 128
MESH = pl.DeviceIdType.MESH
F32 = jnp.float32
BF16 = jnp.bfloat16
PARTS = 4
Z_AT, Y_AT, X_AT, C_AT, COPIES = 0, 3, 7, 13, 26


def fits(mesh):
    return mesh.shape["pack"] == 8 and mesh.shape["hist"] == 4


def fused(
    rate_ref, q_hbm, k_hbm, v_hbm, g_hbm, users_ref, gain_ref, w_hbm, o_hbm,
    q, k, v, g, w, gated, acc, out, local, final, s_in, s_out, prior, same, rows_last, opened,
    load_sem, send_sem, recv_sem, state_send, state_recv, user_sem,
):
    length, width = q.shape
    depth = w.shape[1]
    quarter, half = depth // 4, depth // 2
    blocks = length // GROUP
    pack, hist = lax.axis_index("pack"), lax.axis_index("hist")
    z, y = pack // 2, lax.rem(pack, 2)
    x, core = hist // 2, lax.rem(hist, 2)
    last_hist = 3

    def pack_of(dz, dy):
        return lax.rem(z + dz + 4, 4) * 2 + (y if dy == 0 else 1 - y)

    y_peer = (pack_of(0, 1), hist)
    x_peer = (pack, (1 - x) * 2 + core)
    c_peer = (pack, x * 2 + 1 - core)
    z_peers = [(pack_of(d, 0), hist) for d in range(1, 4)]

    loads = []
    for i, (src, dst) in enumerate([(k_hbm, k), (v_hbm, v), (q_hbm, q), (g_hbm, g), (w_hbm, w.at[pack])]):
        loads.append(pltpu.make_async_copy(src, dst, load_sem.at[i]))
        loads[-1].start()

    barrier = pltpu.get_barrier_semaphore()
    others = [(pack, lax.rem(hist + d, 4)) for d in range(1, 4)]
    for peer in z_peers + [y_peer] + others:
        pl.semaphore_signal(barrier, inc=1, device_id=peer, device_id_type=MESH)
    pl.semaphore_wait(barrier, len(z_peers) + 1 + len(others))

    users_copy = pltpu.make_async_remote_copy(
        users_ref, prior, user_sem.at[0], user_sem.at[1],
        device_id=(pack, jnp.minimum(hist + 1, last_hist)), device_id_type=MESH,
    )

    @pl.when(hist < last_hist)
    def _():
        users_copy.start()

    my_rows = pl.ds(pl.multiple_of(hist * quarter, quarter), quarter)
    x_rows = pl.ds(pl.multiple_of(((1 - x) * 2 + core) * quarter, quarter), quarter)
    core_rows = pl.ds(pl.multiple_of(core * half, half), half)

    started = []

    def send(at, src, dst, peer):
        copy = pltpu.make_async_remote_copy(
            src, dst, send_sem.at[at], recv_sem.at[at], device_id=peer, device_id_type=MESH
        )
        copy.start()
        started.append(copy)

    def arrived(at, where):
        pltpu.make_async_remote_copy(
            where, where, send_sem.at[at], recv_sem.at[at], device_id=c_peer, device_id_type=MESH
        ).wait_recv()

    for d in (1, 3, 2):
        send(Z_AT + d - 1, w_hbm.at[my_rows], w.at[pack, my_rows], z_peers[d - 1])
    send(Y_AT, w_hbm.at[core_rows], w.at[pack, core_rows], y_peer)

    def part(shard, rows):
        return w.at[shard, rows]

    def on_z(d):
        here = part(pack_of(-d, 0), my_rows)
        arrived(Z_AT + d - 1, here)
        send(X_AT + (d - 1) * 2, here, here, x_peer)
        send(Y_AT + d, here, here, y_peer)
        send(C_AT + Z_AT + d - 1, here, here, c_peer)

    def on_y(d):
        here = part(pack_of(-d, 1), core_rows if d == 0 else my_rows)
        arrived(Y_AT + d, here)
        if d > 0:
            send(X_AT + (d - 1) * 2 + 1, here, here, x_peer)
        send(C_AT + Y_AT + d, here, here, c_peer)

    def on_x(d, dy):
        here = part(pack_of(-d, dy), x_rows)
        at = X_AT + (d - 1) * 2 + dy
        arrived(at, here)
        send(C_AT + at, here, here, c_peer)

    def wait_core(d, dy):
        shard = pack_of(-d, dy)
        if d == 0:
            arrived(C_AT + Y_AT, part(shard, core_rows))
        else:
            arrived(C_AT + (Y_AT + d if dy else Z_AT + d - 1), part(shard, my_rows))
            arrived(C_AT + X_AT + (d - 1) * 2 + dy, part(shard, x_rows))

    square = (GROUP, GROUP)
    row_at = lax.broadcasted_iota(jnp.int32, square, 0)
    col_at = lax.broadcasted_iota(jnp.int32, square, 1)

    def user_row(ref, c):
        return ref[:, c * GROUP:(c + 1) * GROUP].astype(F32)

    def last_of(ref, c):
        return jnp.broadcast_to(user_row(ref, c)[:, GROUP - 1:], (1, GROUP))

    for c in range(blocks):
        across = jnp.broadcast_to(user_row(users_ref, c), square)
        down = across.T
        same[c] = jnp.where(jnp.logical_and(across == down, row_at >= col_at), 1.0, 0.0)
        rows_last[c] = jnp.where(down == last_of(users_ref, c), 1.0, 0.0)
        if c > 0:
            opened[c] = jnp.where(down == last_of(users_ref, c - 1), 1.0, 0.0)

    def log_decay(head):
        return jnp.log1p(-jnp.full((1, HEAD_DIM), rate_ref[head], F32))

    loads[0].wait()
    loads[1].wait()

    def states(head, carry):
        cols = pl.ds(pl.multiple_of(head * HEAD_DIM, HEAD_DIM), HEAD_DIM)
        decay = log_decay(head)
        tail = jnp.exp((GROUP - 1 - row_at).astype(F32) * decay)
        step = jnp.exp(GROUP * decay)
        state = None
        for c in range(blocks):
            events = slice(c * GROUP, (c + 1) * GROUP)
            scaled = (k[events, cols].astype(F32) * (tail * rows_last[c])).astype(BF16)
            own = lax.dot_general(
                scaled, v[events, cols], (((0,), (0,)), ((), ())), preferred_element_type=F32
            )
            if c == 0:
                state = own
            else:
                keep = jnp.where(last_of(users_ref, c) == last_of(users_ref, c - 1), step, 0.0)
                state = keep * state + own
            if c + 1 < blocks:
                local[head, c] = state
            else:
                final[head] = state
        return carry

    heads_part = HEADS // PARTS

    lax.fori_loop(0, HEADS, states, 0)

    @pl.when(hist > 0)
    def _():
        users_copy.wait_recv()

    @pl.when(hist == 0)
    def _():
        prior[...] = jnp.full(prior.shape, -1, jnp.int32)
        s_in[...] = jnp.zeros(s_in.shape, BF16)

    before_all = last_of(prior, blocks - 1)
    down = jnp.broadcast_to(user_row(users_ref, 0), square).T
    opened[0] = jnp.where(down == before_all, 1.0, 0.0)

    def state_copy(i):
        heads = pl.ds(i * heads_part, heads_part)
        return pltpu.make_async_remote_copy(
            s_out.at[heads], s_in.at[heads], state_send.at[i], state_recv.at[i],
            device_id=(pack, jnp.minimum(hist + 1, last_hist)), device_id_type=MESH,
        )

    def pass_on(i):
        @pl.when(hist > 0)
        def _():
            state_copy(i).wait_recv()

        @pl.when(hist < last_hist)
        def _():
            for head in range(i * heads_part, (i + 1) * heads_part):
                whole = jnp.exp(length * log_decay(head))
                keep = jnp.where(last_of(users_ref, blocks - 1) == before_all, whole, 0.0)
                s_out[head] = (keep * s_in[head].astype(F32) + final[head]).astype(BF16)
            state_copy(i).start()

    pass_on(0)
    on_z(1)
    pass_on(1)
    on_y(0)
    on_z(3)
    pass_on(2)
    on_z(2)
    pass_on(3)
    loads[2].wait()
    loads[3].wait()

    def retain(head, carry):
        cols = pl.ds(pl.multiple_of(head * HEAD_DIM, HEAD_DIM), HEAD_DIM)
        decay = log_decay(head)
        within = jnp.exp(jnp.maximum(row_at - col_at, 0).astype(F32) * decay)
        reach = jnp.exp((row_at + 1).astype(F32) * decay)
        gain = gain_ref[:, cols]
        came = s_in[head].astype(F32)
        for c in range(blocks):
            events = slice(c * GROUP, (c + 1) * GROUP)
            qb, vb = q[events, cols], v[events, cols]
            scores = lax.dot_general(
                qb, k[events, cols], (((1,), (1,)), ((), ())), preferred_element_type=F32
            )
            weights = (scores * (within * same[c])).astype(BF16)
            if c == 0:
                entering = s_in[head]
            else:
                keep = jnp.where(last_of(users_ref, c - 1) == before_all, jnp.exp(c * GROUP * decay), 0.0)
                entering = (local[head, c - 1] + keep * came).astype(BF16)
            reached = (qb.astype(F32) * (reach * opened[c])).astype(BF16)
            kept = jnp.dot(
                jnp.concatenate([weights, reached], axis=1),
                jnp.concatenate([vb, entering], axis=0),
                preferred_element_type=F32,
            )
            mean = jnp.mean(kept, axis=1, keepdims=True)
            centred = kept - mean
            variance = jnp.mean(centred * centred, axis=1, keepdims=True)
            normed = centred * lax.rsqrt(variance + 1e-05) * gain
            a = g[events, cols].astype(F32)
            gated[events, cols] = (a / (1.0 + jnp.exp(-a)) * normed).astype(BF16)
        return carry

    events_after = {
        0: [lambda: on_y(1)],
        1: [lambda: on_y(3)],
        2: [lambda: on_y(2)],
        3: [lambda: on_x(1, 0)],
        4: [lambda: on_x(3, 0)],
        5: [lambda: on_x(1, 1)],
        6: [lambda: on_x(3, 1)],
        7: [],
    }
    for i in range(8):
        lax.fori_loop(i * 2, i * 2 + 2, retain, 0)
        for event in events_after[i]:
            event()

    tile = 512

    def project(shards, first=False, last=False):
        def body(j, carry):
            cols = pl.ds(pl.multiple_of(j * tile, tile), tile)
            total = None if first else acc[:, cols]
            for shard in shards:
                rows = pl.ds(pl.multiple_of(shard * depth, depth), depth)
                term = jnp.dot(gated[:, rows], w[shard, :, cols], preferred_element_type=F32)
                total = term if total is None else total + term
            if last:
                out[:, cols] = total.astype(BF16)
            else:
                acc[:, cols] = total
            return carry

        lax.fori_loop(0, width // tile, body, 0)

    loads[4].wait()
    wait_core(0, 1)
    project([pack, pack_of(0, 1)], first=True)
    on_x(2, 0)
    wait_core(1, 0)
    project([pack_of(-1, 0)])
    wait_core(3, 0)
    project([pack_of(-3, 0)])
    wait_core(1, 1)
    project([pack_of(-1, 1)])
    on_x(2, 1)
    wait_core(3, 1)
    project([pack_of(-3, 1)])
    wait_core(2, 0)
    project([pack_of(-2, 0)])
    wait_core(2, 1)
    project([pack_of(-2, 1)], last=True)
    store = pltpu.make_async_copy(out, o_hbm, load_sem.at[0])
    store.start()
    for copy in started:
        copy.wait_send()

    @pl.when(hist < last_hist)
    def _():
        users_copy.wait_send()
        for i in range(PARTS):
            state_copy(i).wait_send()

    store.wait()


def local_fused(queries, keys, values, gates, user_ids, forget_rate, norm_gain, w_out):
    length, width = queries.shape[1:]
    depth = w_out.shape[0]
    blocks = length // GROUP
    here = pl.BlockSpec(memory_space=pl.ANY)
    vmem = pl.BlockSpec(memory_space=pltpu.VMEM)
    big = pltpu.VMEM((length, width), BF16)
    square = (HEAD_DIM, HEAD_DIM)
    mixed = pl.pallas_call(
        fused,
        out_shape=jax.ShapeDtypeStruct((length, width), BF16),
        in_specs=[pl.BlockSpec(memory_space=pltpu.SMEM), here, here, here, here, vmem, vmem, here],
        out_specs=here,
        scratch_shapes=[
            big, big, big, big,
            pltpu.VMEM((width // depth, depth, width), BF16),
            big,
            pltpu.VMEM((length, width), F32),
            big,
            pltpu.VMEM((HEADS, blocks - 1) + square, F32),
            pltpu.VMEM((HEADS,) + square, F32),
            pltpu.VMEM((HEADS,) + square, BF16),
            pltpu.VMEM((HEADS,) + square, BF16),
            pltpu.VMEM((1, length), jnp.int32),
            pltpu.VMEM((blocks, GROUP, GROUP), F32),
            pltpu.VMEM((blocks, GROUP, GROUP), F32),
            pltpu.VMEM((blocks, GROUP, GROUP), F32),
            pltpu.SemaphoreType.DMA((5,)),
            pltpu.SemaphoreType.DMA((COPIES,)),
            pltpu.SemaphoreType.DMA((COPIES,)),
            pltpu.SemaphoreType.DMA((PARTS,)),
            pltpu.SemaphoreType.DMA((PARTS,)),
            pltpu.SemaphoreType.DMA((2,)),
        ],
        compiler_params=pltpu.CompilerParams(
            collective_id=0, has_side_effects=True, vmem_limit_bytes=56 * 1024 * 1024
        ),
        cost_estimate=pl.CostEstimate(
            flops=2 * length * width * (width + 4 * HEAD_DIM), bytes_accessed=12 * length * width, transcendentals=0
        ),
    )(
        forget_rate, queries[0], keys[0], values[0], gates[0], user_ids, norm_gain.reshape(1, width), w_out,
    )
    return mixed[None]


def solution(mesh):
    in_specs = (
        P("pack", "hist", None),
        P("pack", "hist", None),
        P("pack", "hist", None),
        P("pack", "hist", None),
        P("pack", "hist"),
        P(),
        P(),
        P("pack", None),
    )
    out_specs = P("pack", "hist", None)
    local = local_fused if fits(mesh) else local_any
    return jax.shard_map(local, mesh=mesh, in_specs=in_specs, out_specs=out_specs, check_vma=False)
```

```python
import functools

import jax
import jax.numpy as jnp
from jax import lax
from jax.experimental import pallas as pl
from jax.experimental.pallas import tpu as pltpu
from jax.sharding import PartitionSpec as P

HEADS = 16
GROUP = 128


def passed_along(array, axis, by):
    size = lax.axis_size(axis)
    pairs = [(i, i + by) for i in range(size) if 0 <= i + by < size]
    return lax.ppermute(array, axis, pairs)


def carried_in(array, axis, combine, identity):
    size, here = (lax.axis_size(axis), lax.axis_index(axis))
    everything = jax.tree.map(lambda part: lax.all_gather(part, axis), array)
    start = jax.tree.map(
        lambda part, zero: jnp.broadcast_to(jnp.asarray(zero, part.dtype), part.shape),
        array,
        identity,
    )

    def hop(k, before):
        reached = k < here
        new = combine(before, jax.tree.map(lambda part: part[k], everything))
        return jax.tree.map(lambda a, b: jnp.where(reached, a, b), new, before)

    return lax.fori_loop(0, size, hop, start)


def combine_states(earlier, later):
    return (earlier[0] * later[0], later[0][:, None, None] * earlier[1] + later[1])


def local_any(queries, keys, values, gates, user_ids, forget_rate, norm_gain, w_out):
    length = queries.shape[1]
    width = queries.shape[2]
    head_dim = width // HEADS
    blocks = length // GROUP
    log_decay = jnp.log1p(-forget_rate)
    users = user_ids[0]
    before = passed_along(users[length - 1 :], "hist", 1)
    prior = jnp.concatenate([before, users[:-1]])
    place_all = jnp.arange(length, dtype=jnp.int32)
    forced = jnp.logical_and(lax.axis_index("hist") == 0, place_all == 0)
    starts = jnp.logical_or(users != prior, forced).astype(jnp.int32)
    seg = users.reshape(blocks, GROUP)
    start_blk = starts.reshape(blocks, GROUP)
    q_blk = queries[0].reshape(blocks, GROUP, HEADS, head_dim)
    k_blk = keys[0].reshape(blocks, GROUP, HEADS, head_dim)
    v_blk = values[0].reshape(blocks, GROUP, HEADS, head_dim)
    place = jnp.arange(GROUP, dtype=jnp.int32)
    diff = place[:, None] - place[None, :]
    causal = diff >= 0
    lag = jnp.where(causal, diff, 0).astype(jnp.float32)
    decay = jnp.exp(lag[None] * log_decay[:, None, None])
    mask = jnp.logical_and(seg[:, :, None] == seg[:, None, :], causal[None])
    scores = jnp.einsum("nthd,nshd->nhts", q_blk, k_blk, preferred_element_type=jnp.float32)
    weights = jnp.where(mask[:, None], scores * decay[None], 0.0).astype(jnp.bfloat16)
    inner = jnp.einsum("nhts,nshd->nthd", weights, v_blk, preferred_element_type=jnp.float32)
    tail = jnp.exp((GROUP - 1 - place).astype(jnp.float32)[None, :] * log_decay[:, None])
    keep_rows = (seg == seg[:, -1:]).astype(jnp.float32)
    scaled = (k_blk * (keep_rows[:, :, None] * tail.T[None])[..., None]).astype(jnp.bfloat16)
    own = jnp.einsum("nshd,nshe->nhde", scaled, v_blk, preferred_element_type=jnp.float32)
    any_start = jnp.max(start_blk, axis=1) > 0
    keep = jnp.where(any_start[:, None], 0.0, jnp.exp(GROUP * log_decay)[None, :])

    def advance(state, item):
        keep_c, own_c = item
        return (keep_c[:, None, None] * state + own_c, state)

    zero_state = jnp.zeros((HEADS, head_dim, head_dim), jnp.float32)
    local_final, local_enter = lax.scan(advance, zero_state, (keep, own))
    products = [jnp.ones((HEADS,), jnp.float32)]
    for c in range(blocks - 1):
        products.append(products[-1] * keep[c])
    keep_before = jnp.stack(products)
    keep_device = keep_before[-1] * keep[-1]
    identity = (
        jnp.ones((HEADS,), jnp.float32),
        jnp.zeros((HEADS, head_dim, head_dim), jnp.float32),
    )
    incoming = carried_in((keep_device, local_final), "hist", combine_states, identity)[1]
    entering = (local_enter + keep_before[:, :, None, None] * incoming[None]).astype(jnp.bfloat16)
    ahead = prior.reshape(blocks, GROUP)[:, :1]
    first = starts.reshape(blocks, GROUP)[:, :1]
    open_run = jnp.logical_and(seg == ahead, first == 0).astype(jnp.float32)
    reach = jnp.exp((place + 1).astype(jnp.float32)[:, None] * log_decay[None, :])
    factor = open_run[:, :, None] * reach[None]
    carried = (
        jnp.einsum("nthd,nhde->nthe", q_blk, entering, preferred_element_type=jnp.float32)
        * factor[..., None]
    )
    retained = (inner + carried).reshape(length, HEADS, head_dim)
    mean = jnp.mean(retained, axis=2, keepdims=True)
    centred = retained - mean
    variance = jnp.mean(centred * centred, axis=2, keepdims=True)
    normed = (centred * lax.rsqrt(variance + 1e-05)).reshape(length, width) * norm_gain
    gated = (jax.nn.silu(gates[0].astype(jnp.float32)) * normed).astype(jnp.bfloat16)
    mixed = jnp.dot(
        gated, lax.all_gather(w_out, "pack", axis=0, tiled=True), preferred_element_type=jnp.float32
    ).astype(jnp.bfloat16)
    return mixed[None]


HEAD_DIM = 128
MESH = pl.DeviceIdType.MESH
F32 = jnp.float32
BF16 = jnp.bfloat16
PARTS = 4
A_AT, B_AT, Y0_AT, YA_AT, X1_AT, X2_AT = 0, 4, 8, 10, 13, 16
A_IN, B_IN, CORE, SPARE, COPIES = 0, 4, 20, 40, 56


def fits(mesh):
    return mesh.shape["pack"] == 8 and mesh.shape["hist"] == 4


def fused(
    rate_ref, q_hbm, k_hbm, v_hbm, g_hbm, users_ref, gain_ref, w_hbm, o_hbm,
    q, k, v, g, w, gated, acc, out, local, final, s_in, s_out, prior, same, rows_last, opened,
    load_sem, send_sem, recv_sem, state_send, state_recv, user_sem,
):
    length, width = q.shape
    depth = w.shape[1]
    quarter, half = depth // 4, depth // 2
    blocks = length // GROUP
    pack, hist = lax.axis_index("pack"), lax.axis_index("hist")
    z, y = pack // 2, lax.rem(pack, 2)
    x, core = hist // 2, lax.rem(hist, 2)
    last_hist = 3

    def pack_of(dz, dy):
        return lax.rem(z + dz + 4, 4) * 2 + (y if dy == 0 else 1 - y)

    y_peer = (pack_of(0, 1), hist)
    x_peer = (pack, (1 - x) * 2 + core)
    c_peer = (pack, x * 2 + 1 - core)
    z_peers = [(pack_of(d, 0), hist) for d in range(1, 4)]

    loads = []
    for i, (src, dst) in enumerate([(k_hbm, k), (v_hbm, v), (q_hbm, q), (g_hbm, g), (w_hbm, w.at[pack])]):
        loads.append(pltpu.make_async_copy(src, dst, load_sem.at[i]))
        loads[-1].start()

    barrier = pltpu.get_barrier_semaphore()
    others = [(pack, lax.rem(hist + d, 4)) for d in range(1, 4)]
    for peer in z_peers + [y_peer] + others:
        pl.semaphore_signal(barrier, inc=1, device_id=peer, device_id_type=MESH)
    pl.semaphore_wait(barrier, len(z_peers) + 1 + len(others))

    users_copy = pltpu.make_async_remote_copy(
        users_ref, prior, user_sem.at[0], user_sem.at[1],
        device_id=(pack, jnp.minimum(hist + 1, last_hist)), device_id_type=MESH,
    )

    @pl.when(hist < last_hist)
    def _():
        users_copy.start()

    unit = depth // 8
    base = core * half

    def rows_at(first, count):
        return pl.ds(pl.multiple_of(base + first * unit, unit), count * unit)

    z_rows, z_more, x_own = rows_at(2 * x, 2), rows_at(2 - x, 1), rows_at(3 * x, 1)
    x_in, x_in_own = rows_at(2 - 2 * x, 2), rows_at(3 - 3 * x, 1)
    y_rows = [rows_at(0, 2), rows_at(2, 2)]
    first = jnp.where(z == 0, 1, z - 1)
    third = jnp.where(z < 2, 3, 0)
    sources = [first, 6 - z - first - third, third]

    started = []

    def copy_of(at_send, at, where, peer, src=None):
        return pltpu.make_async_remote_copy(
            where if src is None else src, where, send_sem.at[at_send], recv_sem.at[at],
            device_id=peer, device_id_type=MESH,
        )

    def send(at, where, peer, src=None, when=None, at_send=None):
        copy = copy_of(at if at_send is None else at_send, at, where, peer, src)
        if when is None:
            copy.start()
        else:
            pl.when(when)(copy.start)
        started.append((copy, when))

    def arrived(at, where):
        copy_of(0, at, where, c_peer).wait_recv()

    def part(z_from, dy, rows):
        return w.at[z_from * 2 + (y if dy == 0 else 1 - y), rows]

    z_up = (jnp.minimum(z + 1, 3) * 2 + y, hist)
    z_down = (jnp.maximum(z - 1, 0) * 2 + y, hist)

    def send_z(kind, rows):
        src, where = w_hbm.at[rows], w.at[pack, rows]
        send(kind + z, where, z_up, src, z < 3, SPARE + kind)
        send(kind + z, where, z_down, src, z > 0, SPARE + kind + 1)

    def send_y0(i):
        send(Y0_AT + i, w.at[pack, y_rows[i]], y_peer, w_hbm.at[y_rows[i]])

    def pass_z(kind, o, here):
        z_from = sources[o]
        at_send = SPARE + 8 + kind + o
        send(kind + z_from, here, z_up, None, jnp.logical_and(z_from < z, z < 3), at_send)
        send(kind + z_from, here, z_down, None, jnp.logical_and(z_from > z, z > 0), at_send)

    def on_a(o):
        here = part(sources[o], 0, z_rows)
        arrived(A_AT + sources[o], here)
        pass_z(A_AT, o, here)
        send(YA_AT + o, here, y_peer)
        send(X1_AT + o, part(sources[o], 0, x_own), x_peer)
        send(CORE + A_IN + o, here, c_peer)

    def on_b(o):
        here = part(sources[o], 0, z_more)
        arrived(B_AT + sources[o], here)
        pass_z(B_AT, o, here)
        send(CORE + B_IN + o, here, c_peer)

    def on_y0(i):
        here = part(z, 1, y_rows[i])
        arrived(Y0_AT + i, here)
        send(CORE + Y0_AT + i, here, c_peer)

    def on_ya(o):
        here = part(sources[o], 1, z_rows)
        arrived(YA_AT + o, here)
        send(X2_AT + o, here, x_peer)
        send(CORE + YA_AT + o, here, c_peer)

    def on_x1(o):
        here = part(sources[o], 0, x_in_own)
        arrived(X1_AT + o, here)
        send(CORE + X1_AT + o, here, c_peer)

    def on_x2(o):
        here = part(sources[o], 1, x_in)
        arrived(X2_AT + o, here)
        send(CORE + X2_AT + o, here, c_peer)

    def wait_core(o):
        if o is None:
            for i in range(2):
                arrived(CORE + Y0_AT + i, part(z, 1, y_rows[i]))
            return
        for kind, dy, rows in [
            (A_IN, 0, z_rows), (B_IN, 0, z_more), (X1_AT, 0, x_in_own), (YA_AT, 1, z_rows), (X2_AT, 1, x_in)
        ]:
            arrived(CORE + kind + o, part(sources[o], dy, rows))

    send_z(A_AT, z_rows)
    send_y0(0)

    square = (GROUP, GROUP)
    row_at = lax.broadcasted_iota(jnp.int32, square, 0)
    col_at = lax.broadcasted_iota(jnp.int32, square, 1)

    def user_row(ref, c):
        return ref[:, c * GROUP:(c + 1) * GROUP].astype(F32)

    def last_of(ref, c):
        return jnp.broadcast_to(user_row(ref, c)[:, GROUP - 1:], (1, GROUP))

    for c in range(blocks):
        across = jnp.broadcast_to(user_row(users_ref, c), square)
        down = across.T
        same[c] = jnp.where(jnp.logical_and(across == down, row_at >= col_at), 1.0, 0.0)
        rows_last[c] = jnp.where(down == last_of(users_ref, c), 1.0, 0.0)
        if c > 0:
            opened[c] = jnp.where(down == last_of(users_ref, c - 1), 1.0, 0.0)

    def log_decay(head):
        return jnp.log1p(-jnp.full((1, HEAD_DIM), rate_ref[head], F32))

    loads[0].wait()
    loads[1].wait()

    def states(head, carry):
        cols = pl.ds(pl.multiple_of(head * HEAD_DIM, HEAD_DIM), HEAD_DIM)
        decay = log_decay(head)
        tail = jnp.exp((GROUP - 1 - row_at).astype(F32) * decay)
        step = jnp.exp(GROUP * decay)
        state = None
        for c in range(blocks):
            events = slice(c * GROUP, (c + 1) * GROUP)
            scaled = (k[events, cols].astype(F32) * (tail * rows_last[c])).astype(BF16)
            own = lax.dot_general(
                scaled, v[events, cols], (((0,), (0,)), ((), ())), preferred_element_type=F32
            )
            if c == 0:
                state = own
            else:
                keep = jnp.where(last_of(users_ref, c) == last_of(users_ref, c - 1), step, 0.0)
                state = keep * state + own
            if c + 1 < blocks:
                local[head, c] = state
            else:
                final[head] = state
        return carry

    heads_part = HEADS // PARTS

    def state_copy(i):
        heads = pl.ds(i * heads_part, heads_part)
        return pltpu.make_async_remote_copy(
            s_out.at[heads], s_in.at[heads], state_send.at[i], state_recv.at[i],
            device_id=(pack, jnp.minimum(hist + 1, last_hist)), device_id_type=MESH,
        )

    @pl.when(hist == 0)
    def _():
        prior[...] = jnp.full(prior.shape, -1, jnp.int32)
        s_in[...] = jnp.zeros(s_in.shape, BF16)

    for i in range(PARTS):
        lax.fori_loop(i * heads_part, (i + 1) * heads_part, states, 0)

        @pl.when(hist == 0)
        def _():
            heads = slice(i * heads_part, (i + 1) * heads_part)
            s_out[heads] = final[heads].astype(BF16)
            state_copy(i).start()

    @pl.when(hist > 0)
    def _():
        users_copy.wait_recv()

    before_all = last_of(prior, blocks - 1)
    down = jnp.broadcast_to(user_row(users_ref, 0), square).T
    opened[0] = jnp.where(down == before_all, 1.0, 0.0)

    def pass_on(i, at_hist):
        @pl.when(hist == at_hist)
        def _():
            state_copy(i).wait_recv()
            if at_hist < last_hist:
                for head in range(i * heads_part, (i + 1) * heads_part):
                    whole = jnp.exp(length * log_decay(head))
                    keep = jnp.where(last_of(users_ref, blocks - 1) == before_all, whole, 0.0)
                    s_out[head] = (keep * s_in[head].astype(F32) + final[head]).astype(BF16)
                state_copy(i).start()

    for i in range(PARTS):
        pass_on(i, 1)
    on_a(0)
    send_y0(1)
    pass_on(0, 2)
    pass_on(1, 2)
    pass_on(0, 3)
    loads[2].wait()
    loads[3].wait()

    def retain(head, carry):
        cols = pl.ds(pl.multiple_of(head * HEAD_DIM, HEAD_DIM), HEAD_DIM)
        decay = log_decay(head)
        within = jnp.exp(jnp.maximum(row_at - col_at, 0).astype(F32) * decay)
        reach = jnp.exp((row_at + 1).astype(F32) * decay)
        gain = gain_ref[:, cols]
        came = s_in[head].astype(F32)
        for c in range(blocks):
            events = slice(c * GROUP, (c + 1) * GROUP)
            qb, vb = q[events, cols], v[events, cols]
            scores = lax.dot_general(
                qb, k[events, cols], (((1,), (1,)), ((), ())), preferred_element_type=F32
            )
            weights = (scores * (within * same[c])).astype(BF16)
            if c == 0:
                entering = s_in[head]
            else:
                keep = jnp.where(last_of(users_ref, c - 1) == before_all, jnp.exp(c * GROUP * decay), 0.0)
                entering = (local[head, c - 1] + keep * came).astype(BF16)
            reached = (qb.astype(F32) * (reach * opened[c])).astype(BF16)
            kept = jnp.dot(
                jnp.concatenate([weights, reached], axis=1),
                jnp.concatenate([vb, entering], axis=0),
                preferred_element_type=F32,
            )
            mean = jnp.mean(kept, axis=1, keepdims=True)
            centred = kept - mean
            variance = jnp.mean(centred * centred, axis=1, keepdims=True)
            normed = centred * lax.rsqrt(variance + 1e-05) * gain
            a = g[events, cols].astype(F32)
            gated[events, cols] = (a / (1.0 + jnp.exp(-a)) * normed).astype(BF16)
        return carry

    def send_more():
        send_z(B_AT, z_more)

    events_after = [
        [(on_y0, 0), (pass_on, 2, 2), (pass_on, 3, 2)],
        [(on_a, 1), (on_ya, 0), (send_more,), (pass_on, 1, 3)],
        [(on_x1, 0), (on_a, 2)],
        [(on_ya, 1), (on_y0, 1), (pass_on, 2, 3)],
        [(on_b, 0), (on_x2, 0)],
        [(on_ya, 2), (on_x1, 1), (pass_on, 3, 3)],
        [(on_b, 1), (on_x2, 1)],
        [(on_x1, 2)],
    ]
    for i, events in enumerate(events_after):
        lax.fori_loop(i * 2, i * 2 + 2, retain, 0)
        for event, *which in events:
            event(*which)

    tile = 512

    def project(shards, first=False, last=False):
        def body(j, carry):
            cols = pl.ds(pl.multiple_of(j * tile, tile), tile)
            total = None if first else acc[:, cols]
            for shard in shards:
                rows = pl.ds(pl.multiple_of(shard * depth, depth), depth)
                term = jnp.dot(gated[:, rows], w[shard, :, cols], preferred_element_type=F32)
                total = term if total is None else total + term
            if last:
                out[:, cols] = total.astype(BF16)
            else:
                acc[:, cols] = total
            return carry

        lax.fori_loop(0, width // tile, body, 0)

    def pair(z_from):
        return [z_from * 2 + y, z_from * 2 + 1 - y]

    loads[4].wait()
    wait_core(None)
    project(pair(z), first=True)
    on_b(2)
    wait_core(0)
    project(pair(sources[0]))
    on_x2(2)
    wait_core(1)
    project(pair(sources[1]))
    wait_core(2)
    project(pair(sources[2]), last=True)
    store = pltpu.make_async_copy(out, o_hbm, load_sem.at[0])
    store.start()
    for copy, when in started:
        if when is None:
            copy.wait_send()
        else:
            pl.when(when)(copy.wait_send)

    @pl.when(hist < last_hist)
    def _():
        users_copy.wait_send()
        for i in range(PARTS):
            state_copy(i).wait_send()

    store.wait()


def local_fused(queries, keys, values, gates, user_ids, forget_rate, norm_gain, w_out):
    length, width = queries.shape[1:]
    depth = w_out.shape[0]
    blocks = length // GROUP
    here = pl.BlockSpec(memory_space=pl.ANY)
    vmem = pl.BlockSpec(memory_space=pltpu.VMEM)
    big = pltpu.VMEM((length, width), BF16)
    square = (HEAD_DIM, HEAD_DIM)
    mixed = pl.pallas_call(
        fused,
        out_shape=jax.ShapeDtypeStruct((length, width), BF16),
        in_specs=[pl.BlockSpec(memory_space=pltpu.SMEM), here, here, here, here, vmem, vmem, here],
        out_specs=here,
        scratch_shapes=[
            big, big, big, big,
            pltpu.VMEM((width // depth, depth, width), BF16),
            big,
            pltpu.VMEM((length, width), F32),
            big,
            pltpu.VMEM((HEADS, blocks - 1) + square, F32),
            pltpu.VMEM((HEADS,) + square, F32),
            pltpu.VMEM((HEADS,) + square, BF16),
            pltpu.VMEM((HEADS,) + square, BF16),
            pltpu.VMEM((1, length), jnp.int32),
            pltpu.VMEM((blocks, GROUP, GROUP), F32),
            pltpu.VMEM((blocks, GROUP, GROUP), F32),
            pltpu.VMEM((blocks, GROUP, GROUP), F32),
            pltpu.SemaphoreType.DMA((5,)),
            pltpu.SemaphoreType.DMA((COPIES,)),
            pltpu.SemaphoreType.DMA((COPIES,)),
            pltpu.SemaphoreType.DMA((PARTS,)),
            pltpu.SemaphoreType.DMA((PARTS,)),
            pltpu.SemaphoreType.DMA((2,)),
        ],
        compiler_params=pltpu.CompilerParams(
            collective_id=0, has_side_effects=True, vmem_limit_bytes=56 * 1024 * 1024
        ),
        cost_estimate=pl.CostEstimate(
            flops=2 * length * width * (width + 4 * HEAD_DIM), bytes_accessed=12 * length * width, transcendentals=0
        ),
    )(
        forget_rate, queries[0], keys[0], values[0], gates[0], user_ids, norm_gain.reshape(1, width), w_out,
    )
    return mixed[None]


def solution(mesh):
    in_specs = (
        P("pack", "hist", None),
        P("pack", "hist", None),
        P("pack", "hist", None),
        P("pack", "hist", None),
        P("pack", "hist"),
        P(),
        P(),
        P("pack", None),
    )
    out_specs = P("pack", "hist", None)
    local = local_fused if fits(mesh) else local_any
    return jax.shard_map(local, mesh=mesh, in_specs=in_specs, out_specs=out_specs, check_vma=False)
```
